32 devices in a mesh: seq: 8 (over z, x), head: 4 (over y, core).
Axes of the slice: x: 2, y: 2, z: 4, core: 2. Of those that a mesh axis runs over, the one named last changes fastest.
Arguments:
- queries: bfloat16 [4096, 4096], P(('seq', 'head')), may hold values from -100 to 100
- keys: bfloat16 [4096, 4096], P(('seq', 'head')), may hold values from -6 to 6
- values: bfloat16 [4096, 4096], P(('seq', 'head')), may hold values from -6 to 6
- doc_blocks: int32 [8], replicated, may hold values from 1 to 16, 32 in all
Outputs:
- attended: bfloat16 [4096, 4096], P(('seq', 'head'))
The draws below stay inside these ranges and needn't reach their ends.
Inputs may be any that keep to these rules, and one draw needn't show every extreme that they name: `doc_blocks`: the 8 lengths sum to 32; the longest is 16.
All inputs are finite; a program needn't handle non-finite values.
Results may differ from the reference program's by a relative error of at most 0.0031.
Values may be sent and summed in bfloat16 or wider, within the bound.
A program may use at most 64 MiB of HBM per device.

```python
import math
import jax
import jax.numpy as jnp
import numpy as np
from jax import lax

H = 32
DH = 128
BLOCK = 128
NDOC = 8
TOKENS = 4096
STRETCH = 512
NBLK = 32
N_SEQ = 8


def query_key_pair(key):
    shape = (TOKENS, H * DH)
    query_out = jnp.clip(jax.random.normal(jax.random.fold_in(key, 11), shape, jnp.float32), -6.0, 6.0)
    key_out = jnp.clip(jax.random.normal(jax.random.fold_in(key, 12), shape, jnp.float32), -6.0, 6.0)
    return (query_out, key_out)


def draw_queries(key, part):
    return query_key_pair(key)[0].astype(jnp.bfloat16)


def draw_keys(key, part):
    return query_key_pair(key)[1].astype(jnp.bfloat16)


def block_scale(rng, shape, shards, least, largest):
    level, own = 1.0, jax.random.fold_in(rng, 6)
    for dim, blocks in shards:
        draws = jnp.exp(jax.random.uniform(jax.random.fold_in(own, dim), (blocks,), jnp.float32, least / len(shards), largest / len(shards)))
        level = level * jnp.repeat(draws, shape[dim] // blocks).reshape([-1 if axis == dim else 1 for axis in range(len(shape))])
    return level


def split_up(count, total, limit, slope):
    portions = [(1 << 20) // math.isqrt(standing ** slope) + 1 for standing in range(2, count + 1)]
    surplus, counts = total - limit - (count - 1), [1] * (count - 1)
    while surplus > 0:
        candidates = [i for i in range(count - 1) if counts[i] < limit]
        mass, budget = sum([portions[i] for i in candidates]), surplus
        for i in candidates:
            more = min(limit - counts[i], max(1, budget * portions[i] // mass), surplus)
            counts[i] = counts[i] + more
            surplus = surplus - more
    return np.array([limit] + counts)


def ragged_sizes(rng, amount, total, most, skew):
    if amount == 2:
        one = jax.random.randint(rng, (), max(1, total - most), min(most, total - 1) + 1)
        return jnp.stack([one, total - one])
    tallies = jnp.asarray(split_up(amount, total, most, skew), jnp.int32)
    twos = (amount - 1) // 2
    donor, receiver = tallies[1:1 + 2 * twos:2], tallies[2:2 + 2 * twos:2]
    margin = jnp.minimum(donor - 1, most - receiver)
    shifted = jax.random.randint(jax.random.fold_in(rng, 1), (twos,), 0, 1 << 20) % (margin + 1)
    tallies = tallies.at[1:1 + 2 * twos:2].set(donor - shifted).at[2:2 + 2 * twos:2].set(receiver + shifted)
    return tallies[jax.random.permutation(jax.random.fold_in(rng, 2), amount)]


def normal_values(own_key, shape, scale, limit, cuts=(), kind=jnp.bfloat16):
    entries = scale * jax.random.normal(own_key, shape, jnp.float32)
    if cuts:
        entries = entries * block_scale(own_key, shape, cuts, -0.22, 0.18)
    return jnp.clip(entries, -limit, limit).astype(kind)


def setup_inputs(seed: int = 0) -> dict:
    arg_keys = jax.random.split(jax.random.key(seed), 5)
    return {
        "queries": draw_queries(jax.random.fold_in(arg_keys[4], 71), 0),
        "keys": draw_keys(jax.random.fold_in(arg_keys[4], 71), 0),
        "values": normal_values(arg_keys[2], (TOKENS, H * DH), 1.0, 6.0, ((0, 32),)),
        "doc_blocks": ragged_sizes(arg_keys[3], NDOC, NBLK, NBLK // 2, 2).astype(jnp.int32),
    }


def doc_index(positions, doc_blocks):
    doc_ends = (jnp.cumsum(doc_blocks) * BLOCK).astype(jnp.int32)
    return lax.optimization_barrier(jnp.sum((positions[:, None].astype(jnp.int32) >= doc_ends[None, :-1]).astype(jnp.int32), axis=1)).astype(jnp.int32)

def softmax_part(query_rows, key_rows, value_rows, doc_here):
    stretch_len = query_rows.shape[0]
    row_block = min(512, stretch_len)
    inv_root = DH ** (-0.5)
    key_float = key_rows.astype(jnp.float32)
    value_float = value_rows.astype(jnp.float32)
    key_pos = jnp.arange(stretch_len, dtype=jnp.int32)

    def score_block(index):
        first = (index * row_block).astype(jnp.int32)
        query_block = lax.dynamic_slice_in_dim(query_rows, first, row_block, 0).astype(jnp.float32)
        doc_block = lax.dynamic_slice_in_dim(doc_here, first, row_block, 0)
        query_pos = first + jnp.arange(row_block, dtype=jnp.int32)
        scores = jnp.einsum('qhd,khd->hqk', query_block, key_float, precision=lax.Precision.HIGHEST) * inv_root
        allowed = (key_pos[None, :] <= query_pos[:, None]) & (doc_here[None, :] == doc_block[:, None])
        scores = jnp.where(allowed[None], scores, -1e+30)
        peak = lax.optimization_barrier(jnp.max(scores, axis=-1, keepdims=True))
        expo = jnp.exp(scores - peak)
        weights = (expo / lax.optimization_barrier(jnp.sum(expo, axis=-1, keepdims=True))).astype(jnp.bfloat16)
        return jnp.einsum('hqk,khd->qhd', weights.astype(jnp.float32), value_float, precision=lax.Precision.HIGHEST)
    blocks = lax.map(score_block, jnp.arange(stretch_len // row_block, dtype=jnp.int32))
    return blocks.reshape(stretch_len, query_rows.shape[1], DH)

def reference(queries, keys, values, doc_blocks):
    doc_all = doc_index(jnp.arange(TOKENS, dtype=jnp.int32), doc_blocks).reshape(N_SEQ, STRETCH)
    query_all = queries.reshape(N_SEQ, STRETCH, H, DH)
    key_all = keys.reshape(N_SEQ, STRETCH, H, DH)
    value_all = values.reshape(N_SEQ, STRETCH, H, DH)

    def carry_step(state, inputs):
        running, prev_last = state
        key_stretch, value_stretch, doc_stretch = inputs
        prefix = jnp.where(doc_stretch[0] == prev_last, running, jnp.zeros_like(running))
        tail = (doc_stretch == doc_stretch[-1]).astype(jnp.float32)[:, None, None]
        increment = jnp.einsum('lhd,lhe->hde', key_stretch.astype(jnp.float32) * tail, value_stretch.astype(jnp.float32), precision=lax.Precision.HIGHEST)
        kept = jnp.where(prev_last == doc_stretch[-1], running, jnp.zeros_like(running))
        new_running = (increment + kept).astype(jnp.float32)
        return ((new_running, doc_stretch[-1].astype(jnp.int32)), prefix)
    start_state = (jnp.zeros((H, DH, DH), jnp.float32), jnp.array(-1, dtype=jnp.int32))
    unused, prefixes = lax.scan(carry_step, start_state, (key_all, value_all, doc_all))

    def stretch_out(inputs):
        query_stretch, key_stretch, value_stretch, doc_stretch, prefix = inputs
        linear = jnp.einsum('lhd,hde->lhe', query_stretch.astype(jnp.float32), prefix, precision=lax.Precision.HIGHEST)
        normed = linear * lax.rsqrt(lax.optimization_barrier(jnp.mean(linear * linear, axis=-1, keepdims=True)) + 1e-06)
        normed = normed * (doc_stretch == doc_stretch[0]).astype(jnp.float32)[:, None, None]
        soft = softmax_part(query_stretch, key_stretch, value_stretch, doc_stretch)
        return (soft + normed).astype(jnp.bfloat16)
    outputs = lax.map(stretch_out, (query_all, key_all, value_all, doc_all, prefixes))
    return outputs.reshape(TOKENS, H * DH)
```

```python
import functools

import jax
import jax.numpy as jnp
from jax import lax
from jax.experimental import pallas as pl
from jax.experimental.pallas import tpu as pltpu
from jax.sharding import PartitionSpec as P

H = 32
DH = 128
BLOCK = 128
NDOC = 8
MESH = pl.DeviceIdType.MESH
F32 = jnp.float32
BF16 = jnp.bfloat16


def kernel(n_seq, n_head, tokens, q_hbm, k_hbm, v_hbm, doc_ref, out_hbm,
           q_buf, k_buf, v_buf, o_buf, inc, pair_in, chain_in, chain_out, prefix,
           in_send, in_recv, in_local, pair_send, pair_recv, chain_send, chain_recv,
           out_send, out_recv, out_local):
    heads = H // n_head
    span = n_head * tokens
    chunks = min(4, heads)
    per = heads // chunks
    width = per * DH
    outer = n_seq // 2
    seq, me = lax.axis_index("seq"), lax.axis_index("head")
    z, x = seq // 2, seq % 2
    partner = 2 * z + (1 - x)

    barrier = pltpu.get_barrier_semaphore()

    def greet(to_seq, to_head):
        pl.semaphore_signal(barrier, inc=1, device_id=(to_seq, to_head), device_id_type=MESH)

    for r in range(1, n_head):
        greet(seq, (me + r) % n_head)
    greet(partner, me)

    greet((seq + 2) % n_seq, me)
    greet((seq + n_seq - 2) % n_seq, me)
    pl.semaphore_wait(barrier, n_head + 2)

    mine = pl.ds(pl.multiple_of(me * tokens, tokens), tokens)
    arrays = ((k_hbm, k_buf), (v_hbm, v_buf), (q_hbm, q_buf))

    def columns(owner, chunk):
        return pl.ds(pl.multiple_of(owner * (heads * DH) + chunk * width, DH), width)

    def incoming(a, chunk, r):
        source, target = arrays[a]
        to = (me + r) % n_head
        here = pl.ds(chunk * width, width)
        if r == 0:
            return pltpu.make_async_copy(
                source.at[:, columns(me, chunk)], target.at[mine, here], in_local.at[a, chunk])
        return pltpu.make_async_remote_copy(
            src_ref=source.at[:, columns(to, chunk)], dst_ref=target.at[mine, here],
            send_sem=in_send.at[a, chunk, r], recv_sem=in_recv.at[a, chunk, r],
            device_id=(seq, to), device_id_type=MESH)

    def send_in(a, chunk):
        for r in (2, 3, 1, 0) if n_head == 4 else range(n_head):
            incoming(a, chunk, r).start()

    def wait_in(a, chunk):
        for r in range(n_head):
            copy = incoming(a, chunk, r)
            copy.wait() if r == 0 else copy.wait_recv()

    for chunk in range(chunks):
        send_in(0, chunk)
        send_in(1, chunk)
    for chunk in range(chunks):
        send_in(2, chunk)

    ends, total = [], 0
    for d in range(NDOC - 1):
        total = total + doc_ref[d]
        ends.append(total * BLOCK)

    def doc_of(position):
        found = jnp.zeros_like(position)
        for end in ends:
            found = found + jnp.where(position >= end, 1, 0).astype(jnp.int32)
        return found

    def same(one, other):
        return jnp.where(one == other, 1.0, 0.0).astype(F32)

    base = seq * span
    pair_base = 2 * z * span
    before = doc_of(pair_base - 1)
    first0, last0 = doc_of(pair_base), doc_of(pair_base + span - 1)
    first1, last1 = doc_of(pair_base + span), doc_of(pair_base + 2 * span - 1)
    first_here, last_here = doc_of(base), doc_of(base + span - 1)
    keep_pair = same(last0, last1)
    keep_chain = same(before, last0)
    is_second = jnp.where(x == 1, 1.0, 0.0).astype(F32)
    use_chain = (1.0 - is_second) * same(before, first0) + is_second * same(last0, first1) * keep_chain
    use_pair = is_second * same(last0, first1)

    doc_rows = doc_of(base + lax.broadcasted_iota(jnp.int32, (span, DH), 0))
    tail = doc_rows == last_here
    carried = jnp.where(doc_rows == first_here, 1.0, 0.0).astype(F32)
    doc_cols = doc_of(base + lax.broadcasted_iota(jnp.int32, (1, span), 1))

    def head_columns(head):
        return pl.ds(pl.multiple_of(head * DH, DH), DH)

    def increment(chunk):
        wait_in(0, chunk)
        wait_in(1, chunk)
        for head in range(chunk * per, (chunk + 1) * per):
            keys = k_buf[:, head * DH:(head + 1) * DH]
            keys = jnp.where(tail, keys.astype(F32), 0.0).astype(BF16)
            inc[head] = lax.dot_general(
                keys, v_buf[:, head * DH:(head + 1) * DH], (((0,), (0,)), ((), ())),
                preferred_element_type=F32)

    def some(chunk):
        return pl.ds(chunk * per, per)

    def pair_copy(chunk):
        return pltpu.make_async_remote_copy(
            src_ref=inc.at[some(chunk)], dst_ref=pair_in.at[some(chunk)],
            send_sem=pair_send.at[chunk], recv_sem=pair_recv.at[chunk],
            device_id=(partner, me), device_id_type=MESH)

    def chain_copy(chunk, to):
        return pltpu.make_async_remote_copy(
            src_ref=chain_out.at[some(chunk)], dst_ref=chain_in.at[some(chunk)],
            send_sem=chain_send.at[chunk], recv_sem=chain_recv.at[chunk],
            device_id=(to, me), device_id_type=MESH)

    def forward(chunk):
        pair_copy(chunk).wait_recv()

        @pl.when(z > 0)
        def _():
            chain_copy(chunk, seq - 2).wait_recv()

        @pl.when(z == 0)
        def _():
            chain_in[some(chunk)] = jnp.zeros((per, DH, DH), F32)

        first_inc = is_second * pair_in[some(chunk)] + (1.0 - is_second) * inc[some(chunk)]
        second_inc = is_second * inc[some(chunk)] + (1.0 - is_second) * pair_in[some(chunk)]
        chain = chain_in[some(chunk)]

        @pl.when(z < outer - 1)
        def _():
            chain_out[some(chunk)] = second_inc + keep_pair * (first_inc + keep_chain * chain)
            chain_copy(chunk, seq + 2).start()

        prefix[some(chunk)] = use_pair * first_inc + use_chain * chain

    scale = 1.4426950408889634 * DH ** (-0.5)

    def soft_rows(head, i, start):
        rows = pl.ds(start, BLOCK)
        count = (i + 1) * tokens
        queries = q_buf[rows, head_columns(head)]
        scores = lax.dot_general(
            queries, k_buf[:count, head_columns(head)], (((1,), (1,)), ((), ())),
            preferred_element_type=F32)
        row = start + lax.broadcasted_iota(jnp.int32, (BLOCK, 1), 0)
        doc_here = doc_of(base + row)
        allowed = doc_here == doc_cols[:, :count]
        allowed = allowed & (lax.broadcasted_iota(jnp.int32, (1, count), 1) <= row)
        scores = jnp.where(allowed, scores, -1e30)
        peak = jnp.max(scores, axis=-1, keepdims=True)
        expo = jnp.exp2((scores - peak) * scale)
        norm = 1.0 / jnp.sum(expo, axis=-1, keepdims=True)
        weights = (expo * norm).astype(BF16)
        return jnp.dot(weights, v_buf[:count, head_columns(head)], preferred_element_type=F32)

    def linear_rows(head, start):
        rows = pl.ds(start, BLOCK)
        queries = q_buf[rows, head_columns(head)]
        state = prefix[head]
        high = state.astype(BF16)
        rest = state - high.astype(F32)
        mid = rest.astype(BF16)
        low = (rest - mid.astype(F32)).astype(BF16)
        linear = jnp.dot(queries, high, preferred_element_type=F32) + (
            jnp.dot(queries, mid, preferred_element_type=F32)
            + jnp.dot(queries, low, preferred_element_type=F32))
        normed = linear * lax.rsqrt(jnp.mean(linear * linear, axis=-1, keepdims=True) + 1e-06)
        here = doc_of(base + start + lax.broadcasted_iota(jnp.int32, (BLOCK, DH), 0))
        return normed * jnp.where(here == first_here, 1.0, 0.0).astype(F32)

    def attend(chunk):
        @pl.loop(chunk * per, (chunk + 1) * per)
        def _(head):
            for i in range(n_head):
                def block(start):
                    result = soft_rows(head, i, start) + linear_rows(head, start)
                    o_buf[pl.ds(start, BLOCK), head_columns(head)] = result.astype(BF16)

                if tokens == BLOCK:
                    block(i * tokens)
                else:
                    @pl.loop(0, tokens // BLOCK)
                    def _(r):
                        block(pl.multiple_of(i * tokens + r * BLOCK, BLOCK))

    def outgoing(chunk, r):
        to = (me + r) % n_head
        source = o_buf.at[pl.ds(pl.multiple_of(to * tokens, tokens), tokens), pl.ds(chunk * width, width)]
        target = out_hbm.at[:, columns(me, chunk)]
        if r == 0:
            return pltpu.make_async_copy(source, target, out_local.at[chunk])
        return pltpu.make_async_remote_copy(
            src_ref=source, dst_ref=target,
            send_sem=out_send.at[chunk, r], recv_sem=out_recv.at[chunk, r],
            device_id=(seq, to), device_id_type=MESH)

    for chunk in range(chunks):
        increment(chunk)
        pair_copy(chunk).start()
        if chunk > 0:
            forward(chunk - 1)
    forward(chunks - 1)
    for chunk in range(chunks):
        wait_in(2, chunk)
        attend(chunk)
        for r in (2, 3, 1, 0) if n_head == 4 else range(n_head):
            outgoing(chunk, r).start()

    for chunk in range(chunks):
        for a in range(3):
            for r in range(1, n_head):
                incoming(a, chunk, r).wait_send()
        pair_copy(chunk).wait_send()

        @pl.when(z < outer - 1)
        def _():
            chain_copy(chunk, seq + 2).wait_send()

        outgoing(chunk, 0).wait()
        for r in range(1, n_head):
            outgoing(chunk, r).wait()


def on_device(n_seq, n_head, queries, keys, values, doc_blocks):
    tokens, width = queries.shape
    heads = H // n_head
    span = tokens * n_head
    chunks = min(4, heads)
    states = pltpu.VMEM((heads, DH, DH), F32)
    rows = pltpu.VMEM((span, heads * DH), BF16)
    dma = pltpu.SemaphoreType.DMA
    anywhere = pl.BlockSpec(memory_space=pl.ANY)
    return pl.pallas_call(
        functools.partial(kernel, n_seq, n_head, tokens),
        out_shape=jax.ShapeDtypeStruct((tokens, width), BF16),
        in_specs=[anywhere] * 3 + [pl.BlockSpec(memory_space=pltpu.SMEM)],
        out_specs=anywhere,
        scratch_shapes=[
            rows, rows, rows, rows, states, states, states, states, states,
            dma((3, chunks, n_head)), dma((3, chunks, n_head)), dma((3, chunks)),
            dma((chunks,)), dma((chunks,)), dma((chunks,)), dma((chunks,)),
            dma((chunks, n_head)), dma((chunks, n_head)), dma((chunks,)),
        ],
        compiler_params=pltpu.CompilerParams(
            collective_id=0, has_side_effects=True, vmem_limit_bytes=56 * 1024 * 1024),
        cost_estimate=pl.CostEstimate(
            flops=4 * span * span * heads * DH, bytes_accessed=8 * tokens * width,
            transcendentals=span * span * heads),
    )(queries, keys, values, doc_blocks)


def solution(mesh):
    n_seq, n_head = mesh.shape["seq"], mesh.shape["head"]
    placed = (P(("seq", "head"), None),) * 3 + (P(),)
    return jax.shard_map(
        functools.partial(on_device, n_seq, n_head),
        mesh=mesh, in_specs=placed, out_specs=P(("seq", "head"), None), check_vma=False,
    )
```

```python
import functools

import jax
import jax.numpy as jnp
from jax import lax
from jax.experimental import pallas as pl
from jax.experimental.pallas import tpu as pltpu
from jax.sharding import PartitionSpec as P

H = 32
DH = 128
BLOCK = 128
NDOC = 8
MESH = pl.DeviceIdType.MESH
F32 = jnp.float32
BF16 = jnp.bfloat16


def kernel(n_seq, n_head, tokens, q_hbm, k_hbm, v_hbm, doc_ref, out_hbm,
           q_buf, k_buf, v_buf, o_buf, inc, pair_in, chain_in, chain_out, prefix, bias, carried, soft,
           in_send, in_recv, in_local, pair_send, pair_recv, chain_send, chain_recv,
           out_send, out_recv, out_local):
    heads = H // n_head
    span = n_head * tokens
    chunks = min(4, heads)
    per = heads // chunks
    width = per * DH
    outer = n_seq // 2
    seq, me = lax.axis_index("seq"), lax.axis_index("head")
    z, x = seq // 2, seq % 2
    partner = 2 * z + (1 - x)

    barrier = pltpu.get_barrier_semaphore()

    def greet(to_seq, to_head):
        pl.semaphore_signal(barrier, inc=1, device_id=(to_seq, to_head), device_id_type=MESH)

    for r in range(1, n_head):
        greet(seq, (me + r) % n_head)
    greet(partner, me)

    greet((seq + 2) % n_seq, me)
    greet((seq + n_seq - 2) % n_seq, me)
    pl.semaphore_wait(barrier, n_head + 2)

    mine = pl.ds(pl.multiple_of(me * tokens, tokens), tokens)
    arrays = ((k_hbm, k_buf), (v_hbm, v_buf), (q_hbm, q_buf))

    def columns(owner, chunk):
        return pl.ds(pl.multiple_of(owner * (heads * DH) + chunk * width, DH), width)

    def incoming(a, chunk, r):
        source, target = arrays[a]
        to = (me + r) % n_head
        here = pl.ds(chunk * width, width)
        if r == 0:
            return pltpu.make_async_copy(
                source.at[:, columns(me, chunk)], target.at[mine, here], in_local.at[a, chunk])
        return pltpu.make_async_remote_copy(
            src_ref=source.at[:, columns(to, chunk)], dst_ref=target.at[mine, here],
            send_sem=in_send.at[a, chunk, r], recv_sem=in_recv.at[a, chunk, r],
            device_id=(seq, to), device_id_type=MESH)

    def send_in(a, chunk):
        for r in (2, 3, 1, 0) if n_head == 4 else range(n_head):
            incoming(a, chunk, r).start()

    def wait_in(a, chunk):
        for r in range(n_head):
            copy = incoming(a, chunk, r)
            copy.wait() if r == 0 else copy.wait_recv()

    early = max(chunks - 2, 0)
    for chunk in range(chunks):
        send_in(0, chunk)
        send_in(1, chunk)
        if chunk == early:
            send_in(2, 0)
    for chunk in range(1, chunks):
        send_in(2, chunk)

    ends, total = [], 0
    for d in range(NDOC - 1):
        total = total + doc_ref[d]
        ends.append(total * BLOCK)

    def doc_of(position):
        found = jnp.zeros_like(position)
        for end in ends:
            found = found + jnp.where(position >= end, 1, 0).astype(jnp.int32)
        return found

    def same(one, other):
        return jnp.where(one == other, 1.0, 0.0).astype(F32)

    base = seq * span
    pair_base = 2 * z * span
    before = doc_of(pair_base - 1)
    first0, last0 = doc_of(pair_base), doc_of(pair_base + span - 1)
    first1, last1 = doc_of(pair_base + span), doc_of(pair_base + 2 * span - 1)
    first_here, last_here = doc_of(base), doc_of(base + span - 1)
    keep_pair = same(last0, last1)
    keep_chain = same(before, last0)
    is_second = jnp.where(x == 1, 1.0, 0.0).astype(F32)
    use_chain = (1.0 - is_second) * same(before, first0) + is_second * same(last0, first1) * keep_chain
    use_pair = is_second * same(last0, first1)

    doc_rows = doc_of(base + lax.broadcasted_iota(jnp.int32, (span, DH), 0))
    tail = doc_rows == last_here
    carried[...] = jnp.where(doc_rows == first_here, 1.0, 0.0).astype(F32)
    doc_cols = doc_of(base + lax.broadcasted_iota(jnp.int32, (1, span), 1))
    for i in range(n_head):
        start, count = i * tokens, (i + 1) * tokens
        row = start + lax.broadcasted_iota(jnp.int32, (tokens, 1), 0)
        allowed = doc_of(base + row) == doc_cols[:, :count]
        allowed = allowed & (lax.broadcasted_iota(jnp.int32, (1, count), 1) <= row)
        bias[start:start + tokens, :count] = jnp.where(allowed, 0.0, -1e30).astype(F32)

    def head_columns(head):
        return pl.ds(pl.multiple_of(head * DH, DH), DH)

    def increment(chunk):
        wait_in(0, chunk)
        wait_in(1, chunk)
        for head in range(chunk * per, (chunk + 1) * per):
            keys = k_buf[:, head * DH:(head + 1) * DH]
            keys = jnp.where(tail, keys.astype(F32), 0.0).astype(BF16)
            inc[head] = lax.dot_general(
                keys, v_buf[:, head * DH:(head + 1) * DH], (((0,), (0,)), ((), ())),
                preferred_element_type=F32)

    def some(chunk):
        return pl.ds(chunk * per, per)

    def pair_copy(chunk):
        return pltpu.make_async_remote_copy(
            src_ref=inc.at[some(chunk)], dst_ref=pair_in.at[some(chunk)],
            send_sem=pair_send.at[chunk], recv_sem=pair_recv.at[chunk],
            device_id=(partner, me), device_id_type=MESH)

    def chain_copy(chunk, to):
        return pltpu.make_async_remote_copy(
            src_ref=chain_out.at[some(chunk)], dst_ref=chain_in.at[some(chunk)],
            send_sem=chain_send.at[chunk], recv_sem=chain_recv.at[chunk],
            device_id=(to, me), device_id_type=MESH)

    def forward(chunk):
        pair_copy(chunk).wait_recv()

        @pl.when(z > 0)
        def _():
            chain_copy(chunk, seq - 2).wait_recv()

        @pl.when(z == 0)
        def _():
            chain_in[some(chunk)] = jnp.zeros((per, DH, DH), F32)

        first_inc = is_second * pair_in[some(chunk)] + (1.0 - is_second) * inc[some(chunk)]
        second_inc = is_second * inc[some(chunk)] + (1.0 - is_second) * pair_in[some(chunk)]
        chain = chain_in[some(chunk)]

        @pl.when(z < outer - 1)
        def _():
            chain_out[some(chunk)] = second_inc + keep_pair * (first_inc + keep_chain * chain)
            chain_copy(chunk, seq + 2).start()

        state = use_pair * first_inc + use_chain * chain
        high = state.astype(BF16)
        rest = state - high.astype(F32)
        mid = rest.astype(BF16)
        prefix[0, some(chunk)] = high
        prefix[1, some(chunk)] = mid
        prefix[2, some(chunk)] = (rest - mid.astype(F32)).astype(BF16)

    scale = 1.4426950408889634 * DH ** (-0.5)

    def soft_part(chunk):
        wait_in(2, chunk)

        @pl.loop(chunk * per, (chunk + 1) * per)
        def _(head):
            here = head_columns(head)
            for i in range(n_head):
                start, count = i * tokens, (i + 1) * tokens
                scores = lax.dot_general(
                    q_buf[start:count, here], k_buf[:count, here], (((1,), (1,)), ((), ())),
                    preferred_element_type=F32)
                scores = scores + bias[start:count, :count]
                peak = jnp.max(scores, axis=-1, keepdims=True)
                expo = jnp.exp2((scores - peak) * scale)
                norm = 1.0 / jnp.sum(expo, axis=-1, keepdims=True)
                soft[start:count, head_columns(head - chunk * per)] = jnp.dot(
                    (expo * norm).astype(BF16), v_buf[:count, here], preferred_element_type=F32)

    def linear_part(chunk):
        @pl.loop(chunk * per, (chunk + 1) * per)
        def _(head):
            here = head_columns(head)
            queries = q_buf[:, here]
            linear = jnp.dot(queries, prefix[0, head], preferred_element_type=F32) + (
                jnp.dot(queries, prefix[1, head], preferred_element_type=F32)
                + jnp.dot(queries, prefix[2, head], preferred_element_type=F32))
            normed = linear * lax.rsqrt(jnp.mean(linear * linear, axis=-1, keepdims=True) + 1e-06)
            result = soft[:, head_columns(head - chunk * per)] + normed * carried[...]
            o_buf[:, here] = result.astype(BF16)
            for r in (2, 3, 1, 0) if n_head == 4 else range(n_head):
                outgoing(head, r).start()

    def outgoing(head, r):
        to = (me + r) % n_head
        source = o_buf.at[pl.ds(pl.multiple_of(to * tokens, tokens), tokens), head_columns(head)]
        target = out_hbm.at[:, head_columns(me * heads + head)]
        if r == 0:
            return pltpu.make_async_copy(source, target, out_local.at[head])
        return pltpu.make_async_remote_copy(
            src_ref=source, dst_ref=target,
            send_sem=out_send.at[head, r], recv_sem=out_recv.at[head, r],
            device_id=(seq, to), device_id_type=MESH)

    last = chunks - 1
    for chunk in range(last):
        increment(chunk)
        pair_copy(chunk).start()
        if chunk > 0:
            forward(chunk - 1)
    if last > 1:
        soft_part(0)
        linear_part(0)
    increment(last)
    pair_copy(last).start()
    if last > 0:
        forward(last - 1)
    begin = 1 if last > 1 else 0
    for chunk in range(begin, chunks):
        if chunk < last:
            @pl.when(z == chunk - begin)
            def _():
                forward(last)

        soft_part(chunk)
        if chunk == last:
            @pl.when(z >= last - begin)
            def _():
                forward(last)

        linear_part(chunk)

    for chunk in range(chunks):
        for a in range(3):
            for r in range(1, n_head):
                incoming(a, chunk, r).wait_send()
        pair_copy(chunk).wait_send()

        @pl.when(z < outer - 1)
        def _():
            chain_copy(chunk, seq + 2).wait_send()

    @pl.loop(0, heads)
    def _(head):
        for r in range(n_head):
            outgoing(head, r).wait()


def on_device(n_seq, n_head, queries, keys, values, doc_blocks):
    tokens, width = queries.shape
    heads = H // n_head
    span = tokens * n_head
    chunks = min(4, heads)
    states = pltpu.VMEM((heads, DH, DH), F32)
    rows = pltpu.VMEM((span, heads * DH), BF16)
    dma = pltpu.SemaphoreType.DMA
    anywhere = pl.BlockSpec(memory_space=pl.ANY)
    return pl.pallas_call(
        functools.partial(kernel, n_seq, n_head, tokens),
        out_shape=jax.ShapeDtypeStruct((tokens, width), BF16),
        in_specs=[anywhere] * 3 + [pl.BlockSpec(memory_space=pltpu.SMEM)],
        out_specs=anywhere,
        scratch_shapes=[
            rows, rows, rows, rows, states, states, states, states,
            pltpu.VMEM((3, heads, DH, DH), BF16), pltpu.VMEM((span, span), F32),
            pltpu.VMEM((span, DH), F32), pltpu.VMEM((span, heads // chunks * DH), F32),
            dma((3, chunks, n_head)), dma((3, chunks, n_head)), dma((3, chunks)),
            dma((chunks,)), dma((chunks,)), dma((chunks,)), dma((chunks,)),
            dma((heads, n_head)), dma((heads, n_head)), dma((heads,)),
        ],
        compiler_params=pltpu.CompilerParams(
            collective_id=0, has_side_effects=True, vmem_limit_bytes=56 * 1024 * 1024),
        cost_estimate=pl.CostEstimate(
            flops=4 * span * span * heads * DH, bytes_accessed=8 * tokens * width,
            transcendentals=span * span * heads),
    )(queries, keys, values, doc_blocks)


def solution(mesh):
    n_seq, n_head = mesh.shape["seq"], mesh.shape["head"]
    placed = (P(("seq", "head"), None),) * 3 + (P(),)
    return jax.shard_map(
        functools.partial(on_device, n_seq, n_head),
        mesh=mesh, in_specs=placed, out_specs=P(("seq", "head"), None), check_vma=False,
    )
```

```python
import functools

import jax
import jax.numpy as jnp
from jax import lax
from jax.experimental import pallas as pl
from jax.experimental.pallas import tpu as pltpu
from jax.sharding import PartitionSpec as P

H = 32
DH = 128
BLOCK = 128
NDOC = 8
MESH = pl.DeviceIdType.MESH
F32 = jnp.float32
BF16 = jnp.bfloat16


def kernel(n_seq, n_head, tokens, q_hbm, k_hbm, v_hbm, doc_ref, out_hbm,
           q_buf, k_buf, v_buf, o_buf, inc, pair_in, chain_in, chain_out, prefix, bias, carried, soft,
           in_send, in_recv, in_local, pair_send, pair_recv, chain_send, chain_recv,
           out_send, out_recv, out_local):
    heads = H // n_head
    span = n_head * tokens
    chunks = min(4, heads)
    per = heads // chunks
    width = per * DH
    outer = n_seq // 2
    seq, me = lax.axis_index("seq"), lax.axis_index("head")
    z, x = seq // 2, seq % 2
    partner = 2 * z + (1 - x)

    barrier = pltpu.get_barrier_semaphore()

    def greet(to_seq, to_head):
        pl.semaphore_signal(barrier, inc=1, device_id=(to_seq, to_head), device_id_type=MESH)

    for r in range(1, n_head):
        greet(seq, (me + r) % n_head)
    greet(partner, me)

    greet((seq + 2) % n_seq, me)
    greet((seq + n_seq - 2) % n_seq, me)
    pl.semaphore_wait(barrier, n_head + 2)

    mine = pl.ds(pl.multiple_of(me * tokens, tokens), tokens)
    arrays = ((k_hbm, k_buf), (v_hbm, v_buf), (q_hbm, q_buf))

    def columns(owner, chunk):
        return pl.ds(pl.multiple_of(owner * (heads * DH) + chunk * width, DH), width)

    def incoming(a, chunk, r):
        source, target = arrays[a]
        to = (me + r) % n_head
        here = pl.ds(chunk * width, width)
        if r == 0:
            return pltpu.make_async_copy(
                source.at[:, columns(me, chunk)], target.at[mine, here], in_local.at[a, chunk])
        return pltpu.make_async_remote_copy(
            src_ref=source.at[:, columns(to, chunk)], dst_ref=target.at[mine, here],
            send_sem=in_send.at[a, chunk, r], recv_sem=in_recv.at[a, chunk, r],
            device_id=(seq, to), device_id_type=MESH)

    def send_in(a, chunk):
        for r in (2, 3, 1, 0) if n_head == 4 else range(n_head):
            incoming(a, chunk, r).start()

    def wait_in(a, chunk):
        for r in range(n_head):
            copy = incoming(a, chunk, r)
            copy.wait() if r == 0 else copy.wait_recv()

    groups = [("kv", chunk) for chunk in range(chunks)]
    groups.insert(max(chunks - 1, 2), ("q", 0))
    groups += [("q", chunk) for chunk in range(1, chunks)]

    def send_group(index):
        if index < len(groups):
            kind, chunk = groups[index]
            for a in (0, 1) if kind == "kv" else (2,):
                send_in(a, chunk)

    def wait_group(index):
        kind, chunk = groups[index]
        for a in (0, 1) if kind == "kv" else (2,):
            wait_in(a, chunk)
        send_group(index + 2)

    send_group(0)
    send_group(1)

    ends, total = [], 0
    for d in range(NDOC - 1):
        total = total + doc_ref[d]
        ends.append(total * BLOCK)

    def doc_of(position):
        found = jnp.zeros_like(position)
        for end in ends:
            found = found + jnp.where(position >= end, 1, 0).astype(jnp.int32)
        return found

    def same(one, other):
        return jnp.where(one == other, 1.0, 0.0).astype(F32)

    base = seq * span
    pair_base = 2 * z * span
    before = doc_of(pair_base - 1)
    first0, last0 = doc_of(pair_base), doc_of(pair_base + span - 1)
    first1, last1 = doc_of(pair_base + span), doc_of(pair_base + 2 * span - 1)
    first_here, last_here = doc_of(base), doc_of(base + span - 1)
    keep_pair = same(last0, last1)
    keep_chain = same(before, last0)
    is_second = jnp.where(x == 1, 1.0, 0.0).astype(F32)
    use_chain = (1.0 - is_second) * same(before, first0) + is_second * same(last0, first1) * keep_chain
    use_pair = is_second * same(last0, first1)

    doc_rows = doc_of(base + lax.broadcasted_iota(jnp.int32, (span, DH), 0))
    tail = doc_rows == last_here
    carried[...] = jnp.where(doc_rows == first_here, 1.0, 0.0).astype(F32)
    doc_cols = doc_of(base + lax.broadcasted_iota(jnp.int32, (1, span), 1))
    for i in range(n_head):
        start, count = i * tokens, (i + 1) * tokens
        row = start + lax.broadcasted_iota(jnp.int32, (tokens, 1), 0)
        allowed = doc_of(base + row) == doc_cols[:, :count]
        allowed = allowed & (lax.broadcasted_iota(jnp.int32, (1, count), 1) <= row)
        bias[start:start + tokens, :count] = jnp.where(allowed, 0.0, -1e30).astype(F32)

    def head_columns(head):
        return pl.ds(pl.multiple_of(head * DH, DH), DH)

    def increment(chunk):
        for head in range(chunk * per, (chunk + 1) * per):
            keys = k_buf[:, head * DH:(head + 1) * DH]
            keys = jnp.where(tail, keys.astype(F32), 0.0).astype(BF16)
            inc[head] = lax.dot_general(
                keys, v_buf[:, head * DH:(head + 1) * DH], (((0,), (0,)), ((), ())),
                preferred_element_type=F32)

    def some(chunk):
        return pl.ds(chunk * per, per)

    def pair_copy(chunk):
        return pltpu.make_async_remote_copy(
            src_ref=inc.at[some(chunk)], dst_ref=pair_in.at[some(chunk)],
            send_sem=pair_send.at[chunk], recv_sem=pair_recv.at[chunk],
            device_id=(partner, me), device_id_type=MESH)

    def chain_copy(chunk, to):
        return pltpu.make_async_remote_copy(
            src_ref=chain_out.at[some(chunk)], dst_ref=chain_in.at[some(chunk)],
            send_sem=chain_send.at[chunk], recv_sem=chain_recv.at[chunk],
            device_id=(to, me), device_id_type=MESH)

    def forward(chunk):
        pair_copy(chunk).wait_recv()

        @pl.when(z > 0)
        def _():
            chain_copy(chunk, seq - 2).wait_recv()

        @pl.when(z == 0)
        def _():
            chain_in[some(chunk)] = jnp.zeros((per, DH, DH), F32)

        first_inc = is_second * pair_in[some(chunk)] + (1.0 - is_second) * inc[some(chunk)]
        second_inc = is_second * inc[some(chunk)] + (1.0 - is_second) * pair_in[some(chunk)]
        chain = chain_in[some(chunk)]

        @pl.when(z < outer - 1)
        def _():
            chain_out[some(chunk)] = second_inc + keep_pair * (first_inc + keep_chain * chain)
            chain_copy(chunk, seq + 2).start()

        state = use_pair * first_inc + use_chain * chain
        high = state.astype(BF16)
        rest = state - high.astype(F32)
        mid = rest.astype(BF16)
        prefix[0, some(chunk)] = high
        prefix[1, some(chunk)] = mid
        prefix[2, some(chunk)] = (rest - mid.astype(F32)).astype(BF16)

    scale = 1.4426950408889634 * DH ** (-0.5)

    def soft_part(chunk):
        @pl.loop(chunk * per, (chunk + 1) * per)
        def _(head):
            here = head_columns(head)
            for i in range(n_head):
                start, count = i * tokens, (i + 1) * tokens
                scores = lax.dot_general(
                    q_buf[start:count, here], k_buf[:count, here], (((1,), (1,)), ((), ())),
                    preferred_element_type=F32)
                scores = scores + bias[start:count, :count]
                peak = jnp.max(scores, axis=-1, keepdims=True)
                expo = jnp.exp2((scores - peak) * scale)
                norm = 1.0 / jnp.sum(expo, axis=-1, keepdims=True)
                soft[start:count, head_columns(head - chunk * per)] = jnp.dot(
                    (expo * norm).astype(BF16), v_buf[:count, here], preferred_element_type=F32)

    def linear_part(chunk):
        @pl.loop(chunk * per, (chunk + 1) * per)
        def _(head):
            here = head_columns(head)
            queries = q_buf[:, here]
            linear = jnp.dot(queries, prefix[0, head], preferred_element_type=F32) + (
                jnp.dot(queries, prefix[1, head], preferred_element_type=F32)
                + jnp.dot(queries, prefix[2, head], preferred_element_type=F32))
            normed = linear * lax.rsqrt(jnp.mean(linear * linear, axis=-1, keepdims=True) + 1e-06)
            result = soft[:, head_columns(head - chunk * per)] + normed * carried[...]
            o_buf[:, here] = result.astype(BF16)
            for r in (2, 3, 1, 0) if n_head == 4 else range(n_head):
                outgoing(head, r).start()

    def outgoing(head, r):
        to = (me + r) % n_head
        source = o_buf.at[pl.ds(pl.multiple_of(to * tokens, tokens), tokens), head_columns(head)]
        target = out_hbm.at[:, head_columns(me * heads + head)]
        if r == 0:
            return pltpu.make_async_copy(source, target, out_local.at[head])
        return pltpu.make_async_remote_copy(
            src_ref=source, dst_ref=target,
            send_sem=out_send.at[head, r], recv_sem=out_recv.at[head, r],
            device_id=(seq, to), device_id_type=MESH)

    ready = [groups.index(("kv", chunk)) + 1 for chunk in range(chunks)]
    final = [min(groups.index(("q", chunk + 1)) - 1 if chunk + 1 < chunks else len(groups) - 1, ready[chunk] + 3)
             for chunk in range(chunks)]
    for chunk in range(chunks):
        final[chunk] = max(final[chunk], groups.index(("q", chunk)))
    for index, (kind, chunk) in enumerate(groups):
        wait_group(index)
        if kind == "kv":
            increment(chunk)
            pair_copy(chunk).start()
        else:
            soft_part(chunk)
        for other in range(chunks):
            if ready[other] <= index <= final[other]:
                turn = index - ready[other]

                @pl.when(z >= turn if index == final[other] else z == turn)
                def _():
                    forward(other)

        for other in range(chunks):
            if final[other] == index:
                linear_part(other)

    for chunk in range(chunks):
        for a in range(3):
            for r in range(1, n_head):
                incoming(a, chunk, r).wait_send()
        pair_copy(chunk).wait_send()

        @pl.when(z < outer - 1)
        def _():
            chain_copy(chunk, seq + 2).wait_send()

    @pl.loop(0, heads)
    def _(head):
        for r in range(n_head):
            outgoing(head, r).wait()


def on_device(n_seq, n_head, queries, keys, values, doc_blocks):
    tokens, width = queries.shape
    heads = H // n_head
    span = tokens * n_head
    chunks = min(4, heads)
    states = pltpu.VMEM((heads, DH, DH), F32)
    rows = pltpu.VMEM((span, heads * DH), BF16)
    dma = pltpu.SemaphoreType.DMA
    anywhere = pl.BlockSpec(memory_space=pl.ANY)
    return pl.pallas_call(
        functools.partial(kernel, n_seq, n_head, tokens),
        out_shape=jax.ShapeDtypeStruct((tokens, width), BF16),
        in_specs=[anywhere] * 3 + [pl.BlockSpec(memory_space=pltpu.SMEM)],
        out_specs=anywhere,
        scratch_shapes=[
            rows, rows, rows, rows, states, states, states, states,
            pltpu.VMEM((3, heads, DH, DH), BF16), pltpu.VMEM((span, span), F32),
            pltpu.VMEM((span, DH), F32), pltpu.VMEM((span, heads // chunks * DH), F32),
            dma((3, chunks, n_head)), dma((3, chunks, n_head)), dma((3, chunks)),
            dma((chunks,)), dma((chunks,)), dma((chunks,)), dma((chunks,)),
            dma((heads, n_head)), dma((heads, n_head)), dma((heads,)),
        ],
        compiler_params=pltpu.CompilerParams(
            collective_id=0, has_side_effects=True, vmem_limit_bytes=56 * 1024 * 1024),
        cost_estimate=pl.CostEstimate(
            flops=4 * span * span * heads * DH, bytes_accessed=8 * tokens * width,
            transcendentals=span * span * heads),
    )(queries, keys, values, doc_blocks)


def solution(mesh):
    n_seq, n_head = mesh.shape["seq"], mesh.shape["head"]
    placed = (P(("seq", "head"), None),) * 3 + (P(),)
    return jax.shard_map(
        functools.partial(on_device, n_seq, n_head),
        mesh=mesh, in_specs=placed, out_specs=P(("seq", "head"), None), check_vma=False,
    )
```

```python
import functools

import jax
import jax.numpy as jnp
from jax import lax
from jax.experimental import pallas as pl
from jax.experimental.pallas import tpu as pltpu
from jax.sharding import PartitionSpec as P

H = 32
DH = 128
BLOCK = 128
NDOC = 8
MESH = pl.DeviceIdType.MESH
F32 = jnp.float32
BF16 = jnp.bfloat16


def kernel(n_seq, n_head, tokens, q_hbm, k_hbm, v_hbm, doc_ref, out_hbm,
           q_buf, k_buf, v_buf, o_buf, inc, pair_in, chain_in, chain_out, prefix, bias, carried, soft,
           in_send, in_recv, in_local, pair_send, pair_recv, chain_send, chain_recv,
           out_send, out_recv, out_local):
    heads = H // n_head
    span = n_head * tokens
    chunks = min(4, heads)
    per = heads // chunks
    width = per * DH
    outer = n_seq // 2
    seq, me = lax.axis_index("seq"), lax.axis_index("head")
    z, x = seq // 2, seq % 2
    partner = 2 * z + (1 - x)

    barrier = pltpu.get_barrier_semaphore()

    def greet(to_seq, to_head):
        pl.semaphore_signal(barrier, inc=1, device_id=(to_seq, to_head), device_id_type=MESH)

    for r in range(1, n_head):
        greet(seq, (me + r) % n_head)
    greet(partner, me)

    greet((seq + 2) % n_seq, me)
    greet((seq + n_seq - 2) % n_seq, me)
    pl.semaphore_wait(barrier, n_head + 2)

    mine = pl.ds(pl.multiple_of(me * tokens, tokens), tokens)
    arrays = ((k_hbm, k_buf), (v_hbm, v_buf), (q_hbm, q_buf))

    def columns(owner, chunk):
        return pl.ds(pl.multiple_of(owner * (heads * DH) + chunk * width, DH), width)

    def incoming(a, chunk, r):
        source, target = arrays[a]
        to = (me + r) % n_head
        here = pl.ds(chunk * width, width)
        if r == 0:
            return pltpu.make_async_copy(
                source.at[:, columns(me, chunk)], target.at[mine, here], in_local.at[a, chunk])
        return pltpu.make_async_remote_copy(
            src_ref=source.at[:, columns(to, chunk)], dst_ref=target.at[mine, here],
            send_sem=in_send.at[a, chunk, r], recv_sem=in_recv.at[a, chunk, r],
            device_id=(seq, to), device_id_type=MESH)

    def send_in(a, chunk):
        for r in (2, 3, 1, 0) if n_head == 4 else range(n_head):
            incoming(a, chunk, r).start()

    def wait_in(a, chunk):
        for r in range(n_head):
            copy = incoming(a, chunk, r)
            copy.wait() if r == 0 else copy.wait_recv()

    groups = [("kv", chunk) for chunk in range(chunks)]
    groups += [("q", chunk) for chunk in range(chunks)]

    def send_group(index):
        if index < len(groups):
            kind, chunk = groups[index]
            for a in (0, 1) if kind == "kv" else (2,):
                send_in(a, chunk)

    def wait_group(index):
        kind, chunk = groups[index]
        for a in (0, 1) if kind == "kv" else (2,):
            wait_in(a, chunk)
        send_group(index + 2)

    send_group(0)
    send_group(1)

    ends, total = [], 0
    for d in range(NDOC - 1):
        total = total + doc_ref[d]
        ends.append(total * BLOCK)

    def doc_of(position):
        found = jnp.zeros_like(position)
        for end in ends:
            found = found + jnp.where(position >= end, 1, 0).astype(jnp.int32)
        return found

    def same(one, other):
        return jnp.where(one == other, 1.0, 0.0).astype(F32)

    base = seq * span
    pair_base = 2 * z * span
    before = doc_of(pair_base - 1)
    first0, last0 = doc_of(pair_base), doc_of(pair_base + span - 1)
    first1, last1 = doc_of(pair_base + span), doc_of(pair_base + 2 * span - 1)
    first_here, last_here = doc_of(base), doc_of(base + span - 1)
    keep_pair = same(last0, last1)
    keep_chain = same(before, last0)
    is_second = jnp.where(x == 1, 1.0, 0.0).astype(F32)
    use_chain = (1.0 - is_second) * same(before, first0) + is_second * same(last0, first1) * keep_chain
    use_pair = is_second * same(last0, first1)

    doc_rows = doc_of(base + lax.broadcasted_iota(jnp.int32, (span, DH), 0))
    tail = doc_rows == last_here
    carried[...] = jnp.where(doc_rows == first_here, 1.0, 0.0).astype(F32)
    doc_cols = doc_of(base + lax.broadcasted_iota(jnp.int32, (1, span), 1))
    for i in range(n_head):
        start, count = i * tokens, (i + 1) * tokens
        row = start + lax.broadcasted_iota(jnp.int32, (tokens, 1), 0)
        allowed = doc_of(base + row) == doc_cols[:, :count]
        allowed = allowed & (lax.broadcasted_iota(jnp.int32, (1, count), 1) <= row)
        bias[start:start + tokens, :count] = jnp.where(allowed, 0.0, -1e30).astype(F32)

    def head_columns(head):
        return pl.ds(pl.multiple_of(head * DH, DH), DH)

    def increment(chunk):
        for head in range(chunk * per, (chunk + 1) * per):
            keys = k_buf[:, head * DH:(head + 1) * DH]
            keys = jnp.where(tail, keys.astype(F32), 0.0).astype(BF16)
            inc[head] = lax.dot_general(
                keys, v_buf[:, head * DH:(head + 1) * DH], (((0,), (0,)), ((), ())),
                preferred_element_type=F32)

    def some(chunk):
        return pl.ds(chunk * per, per)

    def pair_copy(chunk):
        return pltpu.make_async_remote_copy(
            src_ref=inc.at[some(chunk)], dst_ref=pair_in.at[some(chunk)],
            send_sem=pair_send.at[chunk], recv_sem=pair_recv.at[chunk],
            device_id=(partner, me), device_id_type=MESH)

    def chain_copy(chunk, to):
        return pltpu.make_async_remote_copy(
            src_ref=chain_out.at[some(chunk)], dst_ref=chain_in.at[some(chunk)],
            send_sem=chain_send.at[chunk], recv_sem=chain_recv.at[chunk],
            device_id=(to, me), device_id_type=MESH)

    def forward(chunk):
        pair_copy(chunk).wait_recv()

        @pl.when(z > 0)
        def _():
            chain_copy(chunk, seq - 2).wait_recv()

        @pl.when(z == 0)
        def _():
            chain_in[some(chunk)] = jnp.zeros((per, DH, DH), F32)

        first_inc = is_second * pair_in[some(chunk)] + (1.0 - is_second) * inc[some(chunk)]
        second_inc = is_second * inc[some(chunk)] + (1.0 - is_second) * pair_in[some(chunk)]
        chain = chain_in[some(chunk)]

        @pl.when(z < outer - 1)
        def _():
            chain_out[some(chunk)] = second_inc + keep_pair * (first_inc + keep_chain * chain)
            chain_copy(chunk, seq + 2).start()

        state = use_pair * first_inc + use_chain * chain
        high = state.astype(BF16)
        rest = state - high.astype(F32)
        mid = rest.astype(BF16)
        prefix[0, some(chunk)] = high
        prefix[1, some(chunk)] = mid
        prefix[2, some(chunk)] = (rest - mid.astype(F32)).astype(BF16)

    scale = 1.4426950408889634 * DH ** (-0.5)

    def soft_part(chunk):
        @pl.loop(chunk * per, (chunk + 1) * per)
        def _(head):
            here = head_columns(head)
            for i in range(n_head):
                start, count = i * tokens, (i + 1) * tokens
                scores = lax.dot_general(
                    q_buf[start:count, here], k_buf[:count, here], (((1,), (1,)), ((), ())),
                    preferred_element_type=F32)
                scores = scores + bias[start:count, :count]
                peak = jnp.max(scores, axis=-1, keepdims=True)
                expo = jnp.exp2((scores - peak) * scale)
                norm = 1.0 / jnp.sum(expo, axis=-1, keepdims=True)
                soft[start:count, head_columns(head - chunk * per)] = jnp.dot(
                    (expo * norm).astype(BF16), v_buf[:count, here], preferred_element_type=F32)

    def linear_part(chunk):
        @pl.loop(chunk * per, (chunk + 1) * per)
        def _(head):
            here = head_columns(head)
            queries = q_buf[:, here]
            linear = jnp.dot(queries, prefix[0, head], preferred_element_type=F32) + (
                jnp.dot(queries, prefix[1, head], preferred_element_type=F32)
                + jnp.dot(queries, prefix[2, head], preferred_element_type=F32))
            normed = linear * lax.rsqrt(jnp.mean(linear * linear, axis=-1, keepdims=True) + 1e-06)
            result = soft[:, head_columns(head - chunk * per)] + normed * carried[...]
            o_buf[:, here] = result.astype(BF16)
            for r in (2, 3, 1, 0) if n_head == 4 else range(n_head):
                outgoing(head, r).start()

    def outgoing(head, r):
        to = (me + r) % n_head
        source = o_buf.at[pl.ds(pl.multiple_of(to * tokens, tokens), tokens), head_columns(head)]
        target = out_hbm.at[:, head_columns(me * heads + head)]
        if r == 0:
            return pltpu.make_async_copy(source, target, out_local.at[head])
        return pltpu.make_async_remote_copy(
            src_ref=source, dst_ref=target,
            send_sem=out_send.at[head, r], recv_sem=out_recv.at[head, r],
            device_id=(seq, to), device_id_type=MESH)

    ready = [groups.index(("kv", chunk)) + 1 for chunk in range(chunks)]
    final = [min(groups.index(("q", chunk + 1)) - 1 if chunk + 1 < chunks else len(groups) - 1, ready[chunk] + 3)
             for chunk in range(chunks)]
    for chunk in range(chunks):
        final[chunk] = max(final[chunk], groups.index(("q", chunk)))
    for index, (kind, chunk) in enumerate(groups):
        wait_group(index)
        for step in ("middle", "work", "end"):
            if step == "work":
                if kind == "kv":
                    increment(chunk)
                    pair_copy(chunk).start()
                else:
                    soft_part(chunk)
                continue
            for other in range(chunks):
                ends = index == final[other]
                if ready[other] <= index <= final[other] and ends == (step == "end"):
                    turn = index - ready[other]

                    @pl.when(z >= turn if ends else z == turn)
                    def _():
                        forward(other)

        for other in range(chunks):
            if final[other] == index:
                linear_part(other)

    for chunk in range(chunks):
        for a in range(3):
            for r in range(1, n_head):
                incoming(a, chunk, r).wait_send()
        pair_copy(chunk).wait_send()

        @pl.when(z < outer - 1)
        def _():
            chain_copy(chunk, seq + 2).wait_send()

    @pl.loop(0, heads)
    def _(head):
        for r in range(n_head):
            outgoing(head, r).wait()


def on_device(n_seq, n_head, queries, keys, values, doc_blocks):
    tokens, width = queries.shape
    heads = H // n_head
    span = tokens * n_head
    chunks = min(4, heads)
    states = pltpu.VMEM((heads, DH, DH), F32)
    rows = pltpu.VMEM((span, heads * DH), BF16)
    dma = pltpu.SemaphoreType.DMA
    anywhere = pl.BlockSpec(memory_space=pl.ANY)
    return pl.pallas_call(
        functools.partial(kernel, n_seq, n_head, tokens),
        out_shape=jax.ShapeDtypeStruct((tokens, width), BF16),
        in_specs=[anywhere] * 3 + [pl.BlockSpec(memory_space=pltpu.SMEM)],
        out_specs=anywhere,
        scratch_shapes=[
            rows, rows, rows, rows, states, states, states, states,
            pltpu.VMEM((3, heads, DH, DH), BF16), pltpu.VMEM((span, span), F32),
            pltpu.VMEM((span, DH), F32), pltpu.VMEM((span, heads // chunks * DH), F32),
            dma((3, chunks, n_head)), dma((3, chunks, n_head)), dma((3, chunks)),
            dma((chunks,)), dma((chunks,)), dma((chunks,)), dma((chunks,)),
            dma((heads, n_head)), dma((heads, n_head)), dma((heads,)),
        ],
        compiler_params=pltpu.CompilerParams(
            collective_id=0, has_side_effects=True, vmem_limit_bytes=56 * 1024 * 1024),
        cost_estimate=pl.CostEstimate(
            flops=4 * span * span * heads * DH, bytes_accessed=8 * tokens * width,
            transcendentals=span * span * heads),
    )(queries, keys, values, doc_blocks)


def solution(mesh):
    n_seq, n_head = mesh.shape["seq"], mesh.shape["head"]
    placed = (P(("seq", "head"), None),) * 3 + (P(),)
    return jax.shard_map(
        functools.partial(on_device, n_seq, n_head),
        mesh=mesh, in_specs=placed, out_specs=P(("seq", "head"), None), check_vma=False,
    )
```

```python
import functools

import jax
import jax.numpy as jnp
from jax import lax
from jax.experimental import pallas as pl
from jax.experimental.pallas import tpu as pltpu
from jax.sharding import PartitionSpec as P

H = 32
DH = 128
BLOCK = 128
NDOC = 8
MESH = pl.DeviceIdType.MESH
F32 = jnp.float32
BF16 = jnp.bfloat16


def kernel(n_seq, n_head, tokens, q_hbm, k_hbm, v_hbm, doc_ref, out_hbm,
           q_buf, k_buf, v_buf, o_buf, inc, pair_in, chain_in, chain_out, prefix, bias, carried, soft,
           in_send, in_recv, in_local, pair_send, pair_recv, chain_send, chain_recv,
           out_send, out_recv, out_local):
    heads = H // n_head
    span = n_head * tokens
    chunks = min(4, heads)
    per = heads // chunks
    width = per * DH
    outer = n_seq // 2
    seq, me = lax.axis_index("seq"), lax.axis_index("head")
    z, x = seq // 2, seq % 2
    partner = 2 * z + (1 - x)

    barrier = pltpu.get_barrier_semaphore()

    def greet(to_seq, to_head):
        pl.semaphore_signal(barrier, inc=1, device_id=(to_seq, to_head), device_id_type=MESH)

    for r in range(1, n_head):
        greet(seq, (me + r) % n_head)
    greet(partner, me)

    greet((seq + 2) % n_seq, me)
    greet((seq + n_seq - 2) % n_seq, me)
    pl.semaphore_wait(barrier, n_head + 2)

    mine = pl.ds(pl.multiple_of(me * tokens, tokens), tokens)
    arrays = ((k_hbm, k_buf), (v_hbm, v_buf), (q_hbm, q_buf))

    def columns(owner, chunk):
        return pl.ds(pl.multiple_of(owner * (heads * DH) + chunk * width, DH), width)

    def incoming(a, chunk, r):
        source, target = arrays[a]
        to = (me + r) % n_head
        here = pl.ds(chunk * width, width)
        if r == 0:
            return pltpu.make_async_copy(
                source.at[:, columns(me, chunk)], target.at[mine, here], in_local.at[a, chunk])
        return pltpu.make_async_remote_copy(
            src_ref=source.at[:, columns(to, chunk)], dst_ref=target.at[mine, here],
            send_sem=in_send.at[a, chunk, r], recv_sem=in_recv.at[a, chunk, r],
            device_id=(seq, to), device_id_type=MESH)

    def send_in(a, chunk):
        for r in (2, 3, 1, 0) if n_head == 4 else range(n_head):
            incoming(a, chunk, r).start()

    def wait_in(a, chunk):
        for r in range(n_head):
            copy = incoming(a, chunk, r)
            copy.wait() if r == 0 else copy.wait_recv()

    groups = [("kv", chunk) for chunk in range(chunks)]
    groups.insert(max(chunks - 1, 2), ("q", 0))
    groups += [("q", chunk) for chunk in range(1, chunks)]

    def send_group(index):
        if index < len(groups):
            kind, chunk = groups[index]
            for a in (0, 1) if kind == "kv" else (2,):
                send_in(a, chunk)

    def wait_group(index):
        kind, chunk = groups[index]
        for a in (0, 1) if kind == "kv" else (2,):
            wait_in(a, chunk)
        send_group(index + 2)

    send_group(0)
    send_group(1)

    ends, total = [], 0
    for d in range(NDOC - 1):
        total = total + doc_ref[d]
        ends.append(total * BLOCK)

    def doc_of(position):
        found = jnp.zeros_like(position)
        for end in ends:
            found = found + jnp.where(position >= end, 1, 0).astype(jnp.int32)
        return found

    def same(one, other):
        return jnp.where(one == other, 1.0, 0.0).astype(F32)

    base = seq * span
    pair_base = 2 * z * span
    before = doc_of(pair_base - 1)
    first0, last0 = doc_of(pair_base), doc_of(pair_base + span - 1)
    first1, last1 = doc_of(pair_base + span), doc_of(pair_base + 2 * span - 1)
    first_here, last_here = doc_of(base), doc_of(base + span - 1)
    keep_pair = same(last0, last1)
    keep_chain = same(before, last0)
    is_second = jnp.where(x == 1, 1.0, 0.0).astype(F32)
    use_chain = (1.0 - is_second) * same(before, first0) + is_second * same(last0, first1) * keep_chain
    use_pair = is_second * same(last0, first1)

    doc_rows = doc_of(base + lax.broadcasted_iota(jnp.int32, (span, DH), 0))
    tail = doc_rows == last_here
    carried[...] = jnp.where(doc_rows == first_here, 1.0, 0.0).astype(F32)
    doc_cols = doc_of(base + lax.broadcasted_iota(jnp.int32, (1, span), 1))
    for i in range(n_head):
        start, count = i * tokens, (i + 1) * tokens
        row = start + lax.broadcasted_iota(jnp.int32, (tokens, 1), 0)
        allowed = doc_of(base + row) == doc_cols[:, :count]
        allowed = allowed & (lax.broadcasted_iota(jnp.int32, (1, count), 1) <= row)
        bias[start:start + tokens, :count] = jnp.where(allowed, 0.0, -1e30).astype(F32)

    def head_columns(head):
        return pl.ds(pl.multiple_of(head * DH, DH), DH)

    def increment(chunk):
        for head in range(chunk * per, (chunk + 1) * per):
            keys = k_buf[:, head * DH:(head + 1) * DH]
            keys = jnp.where(tail, keys.astype(F32), 0.0).astype(BF16)
            inc[head] = lax.dot_general(
                keys, v_buf[:, head * DH:(head + 1) * DH], (((0,), (0,)), ((), ())),
                preferred_element_type=F32)

    def some(chunk):
        return pl.ds(chunk * per, per)

    def pair_copy(chunk):
        return pltpu.make_async_remote_copy(
            src_ref=inc.at[some(chunk)], dst_ref=pair_in.at[some(chunk)],
            send_sem=pair_send.at[chunk], recv_sem=pair_recv.at[chunk],
            device_id=(partner, me), device_id_type=MESH)

    def chain_copy(chunk, to):
        return pltpu.make_async_remote_copy(
            src_ref=chain_out.at[some(chunk)], dst_ref=chain_in.at[some(chunk)],
            send_sem=chain_send.at[chunk], recv_sem=chain_recv.at[chunk],
            device_id=(to, me), device_id_type=MESH)

    def forward(chunk):
        pair_copy(chunk).wait_recv()

        @pl.when(z > 0)
        def _():
            chain_copy(chunk, seq - 2).wait_recv()

        @pl.when(z == 0)
        def _():
            chain_in[some(chunk)] = jnp.zeros((per, DH, DH), F32)

        first_inc = is_second * pair_in[some(chunk)] + (1.0 - is_second) * inc[some(chunk)]
        second_inc = is_second * inc[some(chunk)] + (1.0 - is_second) * pair_in[some(chunk)]
        chain = chain_in[some(chunk)]

        @pl.when(z < outer - 1)
        def _():
            chain_out[some(chunk)] = second_inc + keep_pair * (first_inc + keep_chain * chain)
            chain_copy(chunk, seq + 2).start()

        state = use_pair * first_inc + use_chain * chain
        high = state.astype(BF16)
        rest = state - high.astype(F32)
        mid = rest.astype(BF16)
        prefix[0, some(chunk)] = high
        prefix[1, some(chunk)] = mid
        prefix[2, some(chunk)] = (rest - mid.astype(F32)).astype(BF16)

    scale = 1.4426950408889634 * DH ** (-0.5)

    def soft_part(chunk):
        @pl.loop(chunk * per, (chunk + 1) * per)
        def _(head):
            here = head_columns(head)
            for i in range(n_head):
                start, count = i * tokens, (i + 1) * tokens
                scores = lax.dot_general(
                    q_buf[start:count, here], k_buf[:count, here], (((1,), (1,)), ((), ())),
                    preferred_element_type=F32)
                scores = scores + bias[start:count, :count]
                peak = jnp.max(scores, axis=-1, keepdims=True)
                expo = jnp.exp2((scores - peak) * scale)
                norm = 1.0 / jnp.sum(expo, axis=-1, keepdims=True)
                soft[start:count, head_columns(head - chunk * per)] = jnp.dot(
                    (expo * norm).astype(BF16), v_buf[:count, here], preferred_element_type=F32)

    def linear_part(chunk):
        @pl.loop(chunk * per, (chunk + 1) * per)
        def _(head):
            here = head_columns(head)
            queries = q_buf[:, here]
            linear = jnp.dot(queries, prefix[0, head], preferred_element_type=F32) + (
                jnp.dot(queries, prefix[1, head], preferred_element_type=F32)
                + jnp.dot(queries, prefix[2, head], preferred_element_type=F32))
            normed = linear * lax.rsqrt(jnp.mean(linear * linear, axis=-1, keepdims=True) + 1e-06)
            result = soft[:, head_columns(head - chunk * per)] + normed * carried[...]
            o_buf[:, here] = result.astype(BF16)
            for r in (2, 3, 1, 0) if n_head == 4 else range(n_head):
                outgoing(head, r).start()

    def outgoing(head, r):
        to = (me + r) % n_head
        source = o_buf.at[pl.ds(pl.multiple_of(to * tokens, tokens), tokens), head_columns(head)]
        target = out_hbm.at[:, head_columns(me * heads + head)]
        if r == 0:
            return pltpu.make_async_copy(source, target, out_local.at[head])
        return pltpu.make_async_remote_copy(
            src_ref=source, dst_ref=target,
            send_sem=out_send.at[head, r], recv_sem=out_recv.at[head, r],
            device_id=(seq, to), device_id_type=MESH)

    ready = [groups.index(("kv", chunk)) + 1 for chunk in range(chunks)]
    final = [min(groups.index(("q", chunk + 1)) - 1 if chunk + 1 < chunks else len(groups) - 1, ready[chunk] + 3)
             for chunk in range(chunks)]
    for chunk in range(chunks):
        final[chunk] = max(final[chunk], groups.index(("q", chunk)))
    for index, (kind, chunk) in enumerate(groups):
        wait_group(index)
        for step in ("middle", "work", "end"):
            if step == "work":
                if kind == "kv":
                    increment(chunk)
                    pair_copy(chunk).start()
                else:
                    soft_part(chunk)
                continue
            for other in range(chunks):
                ends = index == final[other]
                if ready[other] <= index <= final[other] and (ends or kind == "kv") == (step == "end"):
                    turn = index - ready[other]

                    @pl.when(z >= turn if ends else z == turn)
                    def _():
                        forward(other)

        for other in range(chunks):
            if final[other] == index:
                linear_part(other)

    for chunk in range(chunks):
        for a in range(3):
            for r in range(1, n_head):
                incoming(a, chunk, r).wait_send()
        pair_copy(chunk).wait_send()

        @pl.when(z < outer - 1)
        def _():
            chain_copy(chunk, seq + 2).wait_send()

    @pl.loop(0, heads)
    def _(head):
        for r in range(n_head):
            outgoing(head, r).wait()


def on_device(n_seq, n_head, queries, keys, values, doc_blocks):
    tokens, width = queries.shape
    heads = H // n_head
    span = tokens * n_head
    chunks = min(4, heads)
    states = pltpu.VMEM((heads, DH, DH), F32)
    rows = pltpu.VMEM((span, heads * DH), BF16)
    dma = pltpu.SemaphoreType.DMA
    anywhere = pl.BlockSpec(memory_space=pl.ANY)
    return pl.pallas_call(
        functools.partial(kernel, n_seq, n_head, tokens),
        out_shape=jax.ShapeDtypeStruct((tokens, width), BF16),
        in_specs=[anywhere] * 3 + [pl.BlockSpec(memory_space=pltpu.SMEM)],
        out_specs=anywhere,
        scratch_shapes=[
            rows, rows, rows, rows, states, states, states, states,
            pltpu.VMEM((3, heads, DH, DH), BF16), pltpu.VMEM((span, span), F32),
            pltpu.VMEM((span, DH), F32), pltpu.VMEM((span, heads // chunks * DH), F32),
            dma((3, chunks, n_head)), dma((3, chunks, n_head)), dma((3, chunks)),
            dma((chunks,)), dma((chunks,)), dma((chunks,)), dma((chunks,)),
            dma((heads, n_head)), dma((heads, n_head)), dma((heads,)),
        ],
        compiler_params=pltpu.CompilerParams(
            collective_id=0, has_side_effects=True, vmem_limit_bytes=56 * 1024 * 1024),
        cost_estimate=pl.CostEstimate(
            flops=4 * span * span * heads * DH, bytes_accessed=8 * tokens * width,
            transcendentals=span * span * heads),
    )(queries, keys, values, doc_blocks)


def solution(mesh):
    n_seq, n_head = mesh.shape["seq"], mesh.shape["head"]
    placed = (P(("seq", "head"), None),) * 3 + (P(),)
    return jax.shard_map(
        functools.partial(on_device, n_seq, n_head),
        mesh=mesh, in_specs=placed, out_specs=P(("seq", "head"), None), check_vma=False,
    )
```
